32 devices in a mesh: gy: 2 (over y), gx: 4 (over x, core), dp: 4 (over z).
Axes of the slice: x: 2, y: 2, z: 4, core: 2. Of those that a mesh axis runs over, the one named last changes fastest.
Arguments:
- features: bfloat16 [4, 32, 64, 512], P('dp', 'gy', 'gx'), may hold values from -36 to 36
- gain_first: float32 [512], replicated, may hold values from 0.1 to 1.9
- gain_second: float32 [512], replicated, may hold values from 0.1 to 1.9
- kernel: float32 [31, 31, 512], replicated, may hold values from -0.1875 to 0.1875
- up_weight: bfloat16 [512, 2048], replicated, may hold values from -0.25 to 0.25
- down_weight: bfloat16 [2048, 512], replicated, may hold values from -0.125 to 0.125
- cotangent: bfloat16 [4, 32, 64, 512], P('dp', 'gy', 'gx'), may hold values from -20 to 20
Outputs:
- grad_input: bfloat16 [4, 32, 64, 512], P('dp', 'gy', 'gx')
- grad_up: float32 [2048, 512], P(('gy', 'gx', 'dp'))
- grad_down: float32 [2048, 512], P(('gy', 'gx', 'dp'))
- grad_kernel: float32 [31, 31, 512], replicated
- grad_gain_first: float32 [512], replicated
- grad_gain_second: float32 [512], replicated
The draws below stay inside these ranges and needn't reach their ends.
All inputs are finite; a program needn't handle non-finite values.
Results may differ from the reference program's by a relative error of at most 0.0058.
Values may be sent and summed in bfloat16 or wider, within the bound.
A program may use at most 128 MiB of HBM per device.

```python
import jax
import jax.numpy as jnp
from jax import lax

C = 512
F = 2048
K = 31
B = 4
H = 32
W = 64


def draw_features(key, part):
    key_base = jax.random.fold_in(key, 11)
    key_pix = jax.random.fold_in(key, 12)
    key_chan = jax.random.fold_in(key, 13)
    pixel_scale = jnp.exp(jax.random.uniform(key_pix, (B, H, W, 1), jnp.float32, jnp.log(0.3), jnp.log(3.0)))
    chan_scale = jnp.exp(jax.random.uniform(key_chan, (C,), jnp.float32, jnp.log(0.3), jnp.log(3.0)))
    base = jnp.clip(jax.random.normal(key_base, (B, H, W, C), jnp.float32), -4.0, 4.0)
    return (base * pixel_scale * chan_scale).astype(jnp.bfloat16)


def draw_cotangent(key, part):
    key_base = jax.random.fold_in(key, 21)
    row_pos = jnp.arange(H, dtype=jnp.float32) / max(H - 1, 1)
    col_pos = jnp.arange(W, dtype=jnp.float32) / max(W - 1, 1)
    img_pos = jnp.arange(B, dtype=jnp.float32) / max(B - 1, 1)
    scale = (1.0 + 2.0 * img_pos)[:, None, None, None] * (1.0 + 2.0 * row_pos)[None, :, None, None] * (1.0 + 2.0 * col_pos)[None, None, :, None] / 9.0
    base = jnp.clip(jax.random.normal(key_base, (B, H, W, C), jnp.float32), -4.0, 4.0)
    return (base * scale).astype(jnp.bfloat16)


def noise(own_key, shape, deviation, most, kind=jnp.bfloat16):
    result = jax.random.normal(own_key, shape, jnp.float32) * deviation
    return jnp.minimum(jnp.maximum(result, -most), most).astype(kind)


def setup_inputs(seed: int = 0) -> dict:
    key_of = jax.random.split(jax.random.key(seed), 8)
    features = draw_features(jax.random.fold_in(key_of[7], 71), 0)
    gain_first = jnp.clip(1.0 + 0.18 * jax.random.normal(key_of[1], (C,), jnp.float32), 0.1, 1.9)
    gain_second = jnp.clip(1.0 + 0.18 * jax.random.normal(key_of[2], (C,), jnp.float32), 0.1, 1.9)
    kernel = noise(key_of[3], (K, K, C), (K * K) ** -0.5, 0.1875, jnp.float32)
    up_weight = noise(key_of[4], (C, F), C ** -0.5, 0.25)
    down_weight = noise(key_of[5], (F, C), F ** -0.5, 0.125)
    cotangent = draw_cotangent(jax.random.fold_in(key_of[7], 71), 0)
    return {"features": features, "gain_first": gain_first, "gain_second": gain_second, "kernel": kernel, "up_weight": up_weight, "down_weight": down_weight, "cotangent": cotangent}


EPS = 1e-06
GELU_C = 0.7978845608028654
GELU_A = 0.044715

def gelu_parts(hidden):
    tangent = jnp.tanh(GELU_C * (hidden + GELU_A * hidden * hidden * hidden))
    value = 0.5 * hidden * (1.0 + tangent)
    slope = 0.5 * (1.0 + tangent) + 0.5 * hidden * (1.0 - tangent * tangent) * GELU_C * (1.0 + 3.0 * GELU_A * hidden * hidden)
    return (value, slope)

def norm_forward(source, gain):
    mean_val = lax.optimization_barrier(jnp.mean(source, axis=-1, keepdims=True))
    centred = source - mean_val
    spread = lax.optimization_barrier(jnp.mean(centred * centred, axis=-1, keepdims=True))
    scale_inv = lax.rsqrt(spread + EPS)
    normed = centred * scale_inv
    return (normed * gain, normed, scale_inv)

def norm_backward(upstream, gain, normed, scale_inv):
    scaled = upstream * gain
    return scale_inv * (scaled - lax.optimization_barrier(jnp.mean(scaled, axis=-1, keepdims=True)) - normed * lax.optimization_barrier(jnp.mean(scaled * normed, axis=-1, keepdims=True)))

def conv_parts(conv_in, grad_conv, kernel):
    rows = conv_in.shape[1]
    cols = conv_in.shape[2]
    side = kernel.shape[0]
    reach = side // 2
    pad_rows = rows + 2 * reach
    pad_cols = cols + 2 * reach
    shape_two = (pad_rows, pad_cols)
    kernel_hat = jnp.fft.rfft2(kernel, s=shape_two, axes=(0, 1))

    def one_image(pair):
        image_in, image_grad = pair
        padded_in = jnp.pad(image_in, ((reach, reach), (reach, reach), (0, 0)))
        padded_grad = jnp.pad(image_grad, ((reach, reach), (reach, reach), (0, 0)))
        in_hat = jnp.fft.rfft2(padded_in, axes=(0, 1))
        grad_hat = jnp.fft.rfft2(padded_grad, axes=(0, 1))
        zero_grad_hat = jnp.fft.rfft2(image_grad, s=shape_two, axes=(0, 1))
        forward = jnp.fft.irfft2(in_hat * jnp.conj(kernel_hat), s=shape_two, axes=(0, 1))[:rows, :cols]
        backward = jnp.fft.irfft2(grad_hat * kernel_hat, s=shape_two, axes=(0, 1))[2 * reach:2 * reach + rows, 2 * reach:2 * reach + cols]
        cross = in_hat * jnp.conj(zero_grad_hat)
        return (forward, backward, cross)
    forward, backward, cross = lax.map(one_image, (conv_in, grad_conv))
    taps = jnp.fft.irfft2(lax.optimization_barrier(jnp.sum(cross, axis=0)), s=shape_two, axes=(0, 1))[:side, :side]
    return (forward, backward, taps)

def conv_forward(conv_in, kernel):
    rows = conv_in.shape[1]
    cols = conv_in.shape[2]
    side = kernel.shape[0]
    reach = side // 2
    shape_two = (rows + 2 * reach, cols + 2 * reach)
    kernel_hat = jnp.fft.rfft2(kernel, s=shape_two, axes=(0, 1))

    def one_image(image_in):
        padded_in = jnp.pad(image_in, ((reach, reach), (reach, reach), (0, 0)))
        in_hat = jnp.fft.rfft2(padded_in, axes=(0, 1))
        return jnp.fft.irfft2(in_hat * jnp.conj(kernel_hat), s=shape_two, axes=(0, 1))[:rows, :cols]
    return lax.map(one_image, conv_in)

def reference(features, gain_first, gain_second, kernel, up_weight, down_weight, cotangent):
    channels = features.shape[-1]
    inputs = features.astype(jnp.float32)
    first, normed_first, inv_first = norm_forward(inputs, gain_first)
    conv_in = first.astype(jnp.bfloat16)
    conv_wide = conv_in.astype(jnp.float32)
    conv_out = conv_forward(conv_wide, kernel)
    mixed = inputs + conv_out
    second, normed_second, inv_second = norm_forward(mixed, gain_second)
    mlp_in = second.astype(jnp.bfloat16).reshape(-1, channels)
    hidden = jnp.dot(mlp_in, up_weight, preferred_element_type=jnp.float32)
    value, slope = gelu_parts(hidden)
    activated = value.astype(jnp.bfloat16)
    upstream = cotangent.reshape(-1, channels)
    grad_act = lax.dot_general(upstream, down_weight, (((1,), (1,)), ((), ())), preferred_element_type=jnp.float32)
    grad_hidden = (grad_act * slope).astype(jnp.bfloat16)
    grad_normed = lax.dot_general(grad_hidden, up_weight, (((1,), (1,)), ((), ())), preferred_element_type=jnp.float32).reshape(mixed.shape)
    grad_mixed = cotangent.astype(jnp.float32) + norm_backward(grad_normed, gain_second, normed_second, inv_second)
    grad_conv = grad_mixed.astype(jnp.bfloat16)
    unused, grad_source, grad_taps = conv_parts(conv_wide, grad_conv.astype(jnp.float32), kernel)
    grad_input = (grad_mixed + norm_backward(grad_source, gain_first, normed_first, inv_first)).astype(jnp.bfloat16)
    grad_up = lax.dot_general(grad_hidden, mlp_in, (((0,), (0,)), ((), ())), preferred_element_type=jnp.float32) / H
    grad_down = lax.dot_general(activated, upstream, (((0,), (0,)), ((), ())), preferred_element_type=jnp.float32) / H
    grad_kernel = grad_taps / H
    grad_gain_first = lax.optimization_barrier(jnp.sum(grad_source * normed_first, axis=(0, 1, 2))) / H
    grad_gain_second = lax.optimization_barrier(jnp.sum(grad_normed * normed_second, axis=(0, 1, 2))) / H
    return (grad_input, grad_up, grad_down, grad_kernel, grad_gain_first, grad_gain_second)
```

```python
import jax
import jax.numpy as jnp
import numpy as np
from jax import lax
from jax.sharding import PartitionSpec as P

EPS = 1e-06
GELU_C = 0.7978845608028654
GELU_A = 0.044715


def padded_2(x, sides, width):
    for axis, dim in sides:
        size, length = (lax.axis_size(axis), x.shape[dim])
        up = [(i, (i + 1) % size) for i in range(size - 1)]
        down = [(j, i) for i, j in up]
        last = lax.slice_in_dim(x, length - width, length, axis=dim)
        initial = lax.slice_in_dim(x, 0, width, axis=dim)
        before = lax.ppermute(last, axis, up)
        after = lax.ppermute(initial, axis, down)
        x = jnp.concatenate([before, x, after], axis=dim)
    return x


def gelu_parts(hidden):
    tangent = jnp.tanh(GELU_C * (hidden + GELU_A * hidden * hidden * hidden))
    value = 0.5 * hidden * (1.0 + tangent)
    slope = 0.5 * (1.0 + tangent) + 0.5 * hidden * (1.0 - tangent * tangent) * GELU_C * (
        1.0 + 3.0 * GELU_A * hidden * hidden
    )
    return (value, slope)


def norm_forward(source, gain):
    mean_val = jnp.mean(source, axis=-1, keepdims=True)
    centred = source - mean_val
    spread = jnp.mean(centred * centred, axis=-1, keepdims=True)
    scale_inv = lax.rsqrt(spread + EPS)
    normed = centred * scale_inv
    return (normed * gain, normed, scale_inv)


def norm_backward(upstream, gain, normed, scale_inv):
    scaled = upstream * gain
    return scale_inv * (
        scaled
        - jnp.mean(scaled, axis=-1, keepdims=True)
        - normed * jnp.mean(scaled * normed, axis=-1, keepdims=True)
    )


def extend(source, reach):
    return padded_2(source, (("gy", 1), ("gx", 2)), reach)


def transform_tables(tile_rows, tile_cols, side):
    rows, cols = tile_rows + side - 1, tile_cols + side - 1
    freqs, weight = [], []
    for fx in range(cols // 2 + 1):
        self_paired = 2 * fx % cols == 0
        for fy in range(rows // 2 + 1 if self_paired else rows):
            freqs.append((fy, fx))
            alone = self_paired and 2 * fy % rows == 0
            weight.append((1.0 if alone else 2.0) / (rows * cols))
    freqs = np.array(freqs)

    def table(row_ids, col_ids):
        angle = 2 * np.pi * (
            (freqs[:, :1] * row_ids % rows)[:, :, None] / rows
            + (freqs[:, 1:] * col_ids % cols)[:, None, :] / cols
        )
        angle = angle.reshape(len(freqs), -1)
        return jnp.asarray(np.concatenate([np.cos(angle), -np.sin(angle)]), jnp.bfloat16)

    whole = table(np.arange(rows), np.arange(cols))
    corner = table(np.arange(tile_rows), np.arange(tile_cols))
    shifted = table(np.arange(tile_rows) + side - 1, np.arange(tile_cols) + side - 1)
    taps = table(np.arange(side), np.arange(side))
    return whole, corner, shifted, taps, np.array(weight, np.float32)[:, None]


def forward_transform(table, values):
    out = jnp.einsum("fp,bpc->bfc", table, values, preferred_element_type=jnp.float32)
    count = table.shape[0] // 2
    return out[:, :count], out[:, count:]


def inverse_transform(table, real, imag):
    spectrum = jnp.concatenate([real, imag], axis=1).astype(jnp.bfloat16)
    return jnp.einsum("fp,bfc->bpc", table, spectrum, preferred_element_type=jnp.float32)


def flat(values):
    return values.reshape(values.shape[0], -1, values.shape[3])


def local(features, gain_first, gain_second, kernel, up_weight, down_weight, cotangent):
    channels = features.shape[3]
    tile_rows = features.shape[1]
    tile_cols = features.shape[2]
    side = kernel.shape[0]
    reach = side // 2
    inputs = features.astype(jnp.float32)
    first, normed_first, inv_first = norm_forward(inputs, gain_first)
    conv_in = first.astype(jnp.bfloat16)
    padded_in = extend(conv_in, reach)
    whole, corner, shifted, tap_table, weight = transform_tables(tile_rows, tile_cols, side)
    kernel_real, kernel_imag = forward_transform(
        tap_table, kernel.reshape(1, side * side, channels).astype(jnp.bfloat16)
    )
    in_real, in_imag = forward_transform(whole, flat(padded_in))
    conv_out = inverse_transform(
        corner,
        weight * (in_real * kernel_real + in_imag * kernel_imag),
        weight * (in_imag * kernel_real - in_real * kernel_imag),
    ).reshape(inputs.shape)
    mixed = inputs + conv_out
    second, normed_second, inv_second = norm_forward(mixed, gain_second)
    mlp_in = second.astype(jnp.bfloat16).reshape(-1, channels)
    hidden = jnp.dot(mlp_in, up_weight, preferred_element_type=jnp.float32)
    value, slope = gelu_parts(hidden)
    activated = value.astype(jnp.bfloat16)
    upstream = cotangent.reshape(-1, channels)
    grad_act = lax.dot_general(
        upstream, down_weight, (((1,), (1,)), ((), ())), preferred_element_type=jnp.float32
    )
    grad_hidden = (grad_act * slope).astype(jnp.bfloat16)
    up_rows = lax.dot_general(
        grad_hidden, mlp_in, (((0,), (0,)), ((), ())), preferred_element_type=jnp.float32
    )
    down_rows = lax.dot_general(
        activated, upstream, (((0,), (0,)), ((), ())), preferred_element_type=jnp.float32
    )
    summed = lax.psum_scatter(
        jnp.concatenate([up_rows, down_rows], axis=1),
        ("gy", "gx", "dp"),
        scatter_dimension=0,
        tiled=True,
    )
    grad_normed = lax.dot_general(
        grad_hidden, up_weight, (((1,), (1,)), ((), ())), preferred_element_type=jnp.float32
    ).reshape(mixed.shape)
    grad_mixed = cotangent.astype(jnp.float32) + norm_backward(
        grad_normed, gain_second, normed_second, inv_second
    )
    grad_conv = grad_mixed.astype(jnp.bfloat16)
    padded_grad = extend(grad_conv, reach)
    tile_real, tile_imag = forward_transform(corner, flat(grad_conv))
    grad_taps = inverse_transform(
        tap_table,
        weight * jnp.sum(in_real * tile_real + in_imag * tile_imag, axis=0, keepdims=True),
        weight * jnp.sum(in_imag * tile_real - in_real * tile_imag, axis=0, keepdims=True),
    ).reshape(side, side, channels)
    grad_real, grad_imag = forward_transform(whole, flat(padded_grad))
    grad_source = inverse_transform(
        shifted,
        weight * (grad_real * kernel_real - grad_imag * kernel_imag),
        weight * (grad_real * kernel_imag + grad_imag * kernel_real),
    ).reshape(inputs.shape)
    grad_input = (
        grad_mixed + norm_backward(grad_source, gain_first, normed_first, inv_first)
    ).astype(jnp.bfloat16)
    small_sums = lax.psum(
        (
            grad_taps,
            jnp.sum(grad_source * normed_first, axis=(0, 1, 2)),
            jnp.sum(grad_normed * normed_second, axis=(0, 1, 2)),
        ),
        ("gy", "gx", "dp"),
    )
    divisor = tile_rows * lax.axis_size("gy")
    return (
        grad_input,
        summed[:, :channels] / divisor,
        summed[:, channels:] / divisor,
        small_sums[0] / divisor,
        small_sums[1] / divisor,
        small_sums[2] / divisor,
    )


def solution(mesh):
    in_specs = (P("dp", "gy", "gx", None), P(), P(), P(), P(), P(), P("dp", "gy", "gx", None))
    out_specs = (
        P("dp", "gy", "gx", None),
        P(("gy", "gx", "dp"), None),
        P(("gy", "gx", "dp"), None),
        P(),
        P(),
        P(),
    )
    return jax.shard_map(local, mesh=mesh, in_specs=in_specs, out_specs=out_specs, check_vma=False)
```

```python
import jax
import jax.numpy as jnp
import numpy as np
from jax import lax
from jax.sharding import PartitionSpec as P

EPS = 1e-06
GELU_C = 0.7978845608028654
GELU_A = 0.044715


def padded_2(x, sides, width):
    for axis, dim in sides:
        size, length = (lax.axis_size(axis), x.shape[dim])
        up = [(i, (i + 1) % size) for i in range(size - 1)]
        down = [(j, i) for i, j in up]
        last = lax.slice_in_dim(x, length - width, length, axis=dim)
        initial = lax.slice_in_dim(x, 0, width, axis=dim)
        before = lax.ppermute(last, axis, up)
        after = lax.ppermute(initial, axis, down)
        x = jnp.concatenate([before, x, after], axis=dim)
    return x


def gelu_parts(hidden):
    tangent = jnp.tanh(GELU_C * (hidden + GELU_A * hidden * hidden * hidden))
    value = 0.5 * hidden * (1.0 + tangent)
    slope = 0.5 * (1.0 + tangent) + 0.5 * hidden * (1.0 - tangent * tangent) * GELU_C * (
        1.0 + 3.0 * GELU_A * hidden * hidden
    )
    return (value, slope)


def norm_forward(source, gain):
    mean_val = jnp.mean(source, axis=-1, keepdims=True)
    centred = source - mean_val
    spread = jnp.mean(centred * centred, axis=-1, keepdims=True)
    scale_inv = lax.rsqrt(spread + EPS)
    normed = centred * scale_inv
    return (normed * gain, normed, scale_inv)


def norm_backward(upstream, gain, normed, scale_inv):
    scaled = upstream * gain
    return scale_inv * (
        scaled
        - jnp.mean(scaled, axis=-1, keepdims=True)
        - normed * jnp.mean(scaled * normed, axis=-1, keepdims=True)
    )


def extend(source, reach):
    return padded_2(source, (("gy", 1), ("gx", 2)), reach)


def transform_tables(tile_rows, tile_cols, side):
    rows, cols = tile_rows + side - 1, tile_cols + side - 1
    freqs, weight = [], []
    for fx in range(cols // 2 + 1):
        self_paired = 2 * fx % cols == 0
        for fy in range(rows // 2 + 1 if self_paired else rows):
            freqs.append((fy, fx))
            alone = self_paired and 2 * fy % rows == 0
            weight.append((1.0 if alone else 2.0) / (rows * cols))
    freqs = np.array(freqs)

    def table(row_ids, col_ids):
        angle = 2 * np.pi * (
            (freqs[:, :1] * row_ids % rows)[:, :, None] / rows
            + (freqs[:, 1:] * col_ids % cols)[:, None, :] / cols
        )
        angle = angle.reshape(len(freqs), -1)
        return jnp.asarray(np.concatenate([np.cos(angle), -np.sin(angle)]), jnp.bfloat16)

    whole = table(np.arange(rows), np.arange(cols))
    corner = table(np.arange(tile_rows), np.arange(tile_cols))
    shifted = table(np.arange(tile_rows) + side - 1, np.arange(tile_cols) + side - 1)
    taps = table(np.arange(side), np.arange(side))
    return whole, corner, shifted, taps, np.array(weight, np.float32)[:, None]


def forward_transform(table, values):
    out = jnp.einsum("fp,bpc->bfc", table, values, preferred_element_type=jnp.float32)
    count = table.shape[0] // 2
    return out[:, :count], out[:, count:]


def inverse_transform(table, real, imag):
    spectrum = jnp.concatenate([real, imag], axis=1).astype(jnp.bfloat16)
    return jnp.einsum("fp,bfc->bpc", table, spectrum, preferred_element_type=jnp.float32)


def flat(values):
    return values.reshape(values.shape[0], -1, values.shape[3])


def mesh_bits(axes):
    bits = []
    for axis in axes:
        bit = lax.axis_size(axis) // 2
        while bit:
            bits.append((axis, bit))
            bit //= 2
    return bits


def swap(values, axis, bit):
    size = lax.axis_size(axis)
    return lax.ppermute(values, axis, [(i, i ^ bit) for i in range(size)])


def halve(values, bits, order, wire):
    blocks = values.reshape([2] * len(bits) + [values.shape[0] >> len(bits), values.shape[1]])
    left = list(bits)
    for axis, bit in order:
        dim = left.index((axis, bit))
        left.pop(dim)
        mine = (lax.axis_index(axis) // bit) % 2
        sent = lax.dynamic_index_in_dim(blocks, 1 - mine, dim, keepdims=False).astype(wire)
        kept = lax.dynamic_index_in_dim(blocks, mine, dim, keepdims=False)
        blocks = kept + swap(sent, axis, bit).astype(jnp.float32)
    return blocks


def double(block, order):
    for axis, bit in reversed(order):
        other = swap(block, axis, bit)
        low = (lax.axis_index(axis) // bit) % 2 == 0
        block = jnp.concatenate(
            [jnp.where(low, block, other), jnp.where(low, other, block)], axis=0
        )
    return block


def butterfly(values, order):
    for axis, bit in order:
        values = values + swap(values, axis, bit)
    return values


def local(features, gain_first, gain_second, kernel, up_weight, down_weight, cotangent):
    channels = features.shape[3]
    tile_rows = features.shape[1]
    tile_cols = features.shape[2]
    side = kernel.shape[0]
    reach = side // 2
    inputs = features.astype(jnp.float32)
    first, normed_first, inv_first = norm_forward(inputs, gain_first)
    conv_in = first.astype(jnp.bfloat16)
    padded_in = extend(conv_in, reach)
    whole, corner, shifted, tap_table, weight = transform_tables(tile_rows, tile_cols, side)
    kernel_real, kernel_imag = forward_transform(
        tap_table, kernel.reshape(1, side * side, channels).astype(jnp.bfloat16)
    )
    in_real, in_imag = forward_transform(whole, flat(padded_in))
    conv_out = inverse_transform(
        corner,
        weight * (in_real * kernel_real + in_imag * kernel_imag),
        weight * (in_imag * kernel_real - in_real * kernel_imag),
    ).reshape(inputs.shape)
    mixed = inputs + conv_out
    second, normed_second, inv_second = norm_forward(mixed, gain_second)
    mlp_in = second.astype(jnp.bfloat16).reshape(-1, channels)
    hidden = jnp.dot(mlp_in, up_weight, preferred_element_type=jnp.float32)
    value, slope = gelu_parts(hidden)
    activated = value.astype(jnp.bfloat16)
    upstream = cotangent.reshape(-1, channels)
    grad_act = lax.dot_general(
        upstream, down_weight, (((1,), (1,)), ((), ())), preferred_element_type=jnp.float32
    )
    grad_hidden = (grad_act * slope).astype(jnp.bfloat16)
    up_rows = lax.dot_general(
        grad_hidden, mlp_in, (((0,), (0,)), ((), ())), preferred_element_type=jnp.float32
    )
    down_rows = lax.dot_general(
        activated, upstream, (((0,), (0,)), ((), ())), preferred_element_type=jnp.float32
    )
    bits = mesh_bits(("gy", "gx", "dp"))
    along = {axis: [pair for pair in bits if pair[0] == axis][::-1] for axis in ("gy", "gx", "dp")}
    near = along["gx"][:1]
    columns_next = near + along["gx"][1:] + along["gy"] + along["dp"]
    rows_next = near + along["gy"] + along["gx"][1:] + along["dp"]
    up_sum = halve(up_rows, bits, columns_next, jnp.bfloat16)
    down_sum = halve(down_rows, bits, rows_next, jnp.bfloat16)
    grad_normed = lax.dot_general(
        grad_hidden, up_weight, (((1,), (1,)), ((), ())), preferred_element_type=jnp.float32
    ).reshape(mixed.shape)
    grad_mixed = cotangent.astype(jnp.float32) + norm_backward(
        grad_normed, gain_second, normed_second, inv_second
    )
    grad_conv = grad_mixed.astype(jnp.bfloat16)
    padded_grad = extend(grad_conv, reach)
    tile_real, tile_imag = forward_transform(corner, flat(grad_conv))
    grad_taps = inverse_transform(
        tap_table,
        weight * jnp.sum(in_real * tile_real + in_imag * tile_imag, axis=0, keepdims=True),
        weight * jnp.sum(in_imag * tile_real - in_real * tile_imag, axis=0, keepdims=True),
    ).reshape(side, side, channels)
    grad_real, grad_imag = forward_transform(whole, flat(padded_grad))
    grad_source = inverse_transform(
        shifted,
        weight * (grad_real * kernel_real - grad_imag * kernel_imag),
        weight * (grad_real * kernel_imag + grad_imag * kernel_real),
    ).reshape(inputs.shape)
    grad_input = (
        grad_mixed + norm_backward(grad_source, gain_first, normed_first, inv_first)
    ).astype(jnp.bfloat16)
    gain_second_sum = jnp.sum(grad_normed * normed_second, axis=(0, 1, 2))
    taps = side * side
    unit = 8 << len(bits)
    packed = jnp.concatenate(
        [
            grad_taps.reshape(taps, channels),
            gain_second_sum[None],
            jnp.zeros((-(taps + 1) % unit, channels), jnp.float32),
        ]
    )
    small = double(halve(packed, columns_next, columns_next, jnp.float32), columns_next)
    gain_first_sum = butterfly(
        jnp.sum(grad_source * normed_first, axis=(0, 1, 2))[None], columns_next
    )
    divisor = tile_rows * lax.axis_size("gy")
    return (
        grad_input,
        up_sum / divisor,
        down_sum / divisor,
        small[:taps].reshape(side, side, channels) / divisor,
        gain_first_sum[0] / divisor,
        small[taps] / divisor,
    )


def solution(mesh):
    in_specs = (P("dp", "gy", "gx", None), P(), P(), P(), P(), P(), P("dp", "gy", "gx", None))
    out_specs = (
        P("dp", "gy", "gx", None),
        P(("gy", "gx", "dp"), None),
        P(("gy", "gx", "dp"), None),
        P(),
        P(),
        P(),
    )
    return jax.shard_map(local, mesh=mesh, in_specs=in_specs, out_specs=out_specs, check_vma=False)
```

```python
import jax
import jax.numpy as jnp
import numpy as np
from jax import lax
from jax.sharding import PartitionSpec as P

EPS = 1e-06
GELU_C = 0.7978845608028654
GELU_A = 0.044715


def padded_2(x, sides, width):
    for axis, dim in sides:
        size, length = (lax.axis_size(axis), x.shape[dim])
        up = [(i, (i + 1) % size) for i in range(size - 1)]
        down = [(j, i) for i, j in up]
        last = lax.slice_in_dim(x, length - width, length, axis=dim)
        initial = lax.slice_in_dim(x, 0, width, axis=dim)
        before = lax.ppermute(last, axis, up)
        after = lax.ppermute(initial, axis, down)
        x = jnp.concatenate([before, x, after], axis=dim)
    return x


def gelu_parts(hidden):
    tangent = jnp.tanh(GELU_C * (hidden + GELU_A * hidden * hidden * hidden))
    value = 0.5 * hidden * (1.0 + tangent)
    slope = 0.5 * (1.0 + tangent) + 0.5 * hidden * (1.0 - tangent * tangent) * GELU_C * (
        1.0 + 3.0 * GELU_A * hidden * hidden
    )
    return (value, slope)


def norm_forward(source, gain):
    mean_val = jnp.mean(source, axis=-1, keepdims=True)
    centred = source - mean_val
    spread = jnp.mean(centred * centred, axis=-1, keepdims=True)
    scale_inv = lax.rsqrt(spread + EPS)
    normed = centred * scale_inv
    return (normed * gain, normed, scale_inv)


def norm_backward(upstream, gain, normed, scale_inv):
    scaled = upstream * gain
    return scale_inv * (
        scaled
        - jnp.mean(scaled, axis=-1, keepdims=True)
        - normed * jnp.mean(scaled * normed, axis=-1, keepdims=True)
    )


def extend_rows(source, reach):
    return padded_2(source, (("gy", 1),), reach)


def extend_cols(source, reach):
    wide = padded_2(source, (("gx", 2),), reach)
    return jnp.pad(wide, ((0, 0), (0, 0), (0, -wide.shape[2] % 16), (0, 0)))


def transform_tables(tile_rows, tile_cols, side):
    rows, cols = tile_rows + side - 1, tile_cols + side - 1
    freqs, weight = [], []
    for fx in range(cols // 2 + 1):
        self_paired = 2 * fx % cols == 0
        for fy in range(rows // 2 + 1 if self_paired else rows):
            freqs.append((fy, fx))
            alone = self_paired and 2 * fy % rows == 0
            weight.append((1.0 if alone else 2.0) / (rows * cols))
    freqs = np.array(freqs)

    def table(row_ids, col_ids):
        angle = 2 * np.pi * (
            (freqs[:, :1] * row_ids % rows)[:, :, None] / rows
            + (freqs[:, 1:] * col_ids % cols)[:, None, :] / cols
        )
        angle = angle.reshape(len(freqs), -1)
        return jnp.asarray(np.concatenate([np.cos(angle), -np.sin(angle)]), jnp.bfloat16)

    whole = table(np.arange(rows), np.arange(cols + -cols % 16))
    corner = table(np.arange(tile_rows), np.arange(tile_cols))
    shifted = table(np.arange(tile_rows) + side - 1, np.arange(tile_cols) + side - 1)
    taps = table(np.arange(side), np.arange(side))
    return whole, corner, shifted, taps, np.array(weight, np.float32)[:, None]


def forward_transform(table, values):
    out = jnp.einsum("fp,bpc->bfc", table, values, preferred_element_type=jnp.float32)
    count = table.shape[0] // 2
    return out[:, :count], out[:, count:]


def inverse_transform(table, real, imag):
    spectrum = jnp.concatenate([real, imag], axis=1).astype(jnp.bfloat16)
    return jnp.einsum("fp,bfc->bpc", table, spectrum, preferred_element_type=jnp.float32)


def flat(values):
    return values.reshape(values.shape[0], -1, values.shape[3])


def mesh_bits(axes):
    bits = []
    for axis in axes:
        bit = lax.axis_size(axis) // 2
        while bit:
            bits.append((axis, bit))
            bit //= 2
    return bits


def swap(values, axis, bit):
    size = lax.axis_size(axis)
    return lax.ppermute(values, axis, [(i, i ^ bit) for i in range(size)])


def blocked(values, bits):
    return values.reshape([2] * len(bits) + [values.shape[0] >> len(bits), values.shape[1]])


def halve(blocks, bits, order, step, wire):
    axis, bit = order[step]
    dim = [pair for pair in bits if pair not in order[:step]].index((axis, bit))
    mine = (lax.axis_index(axis) // bit) % 2
    sent = lax.dynamic_index_in_dim(blocks, 1 - mine, dim, keepdims=False).astype(wire)
    kept = lax.dynamic_index_in_dim(blocks, mine, dim, keepdims=False)
    return kept + swap(sent, axis, bit).astype(jnp.float32)


def double(block, axis, bit):
    other = swap(block, axis, bit)
    low = (lax.axis_index(axis) // bit) % 2 == 0
    return jnp.concatenate([jnp.where(low, block, other), jnp.where(low, other, block)], axis=0)


def local(features, gain_first, gain_second, kernel, up_weight, down_weight, cotangent):
    channels = features.shape[3]
    tile_rows = features.shape[1]
    tile_cols = features.shape[2]
    side = kernel.shape[0]
    reach = side // 2
    inputs = features.astype(jnp.float32)
    first, normed_first, inv_first = norm_forward(inputs, gain_first)
    conv_in = first.astype(jnp.bfloat16)
    padded_in = extend_cols(extend_rows(conv_in, reach), reach)
    whole, corner, shifted, tap_table, weight = transform_tables(tile_rows, tile_cols, side)
    kernel_real, kernel_imag = forward_transform(
        tap_table, kernel.reshape(1, side * side, channels).astype(jnp.bfloat16)
    )
    in_real, in_imag = forward_transform(whole, flat(padded_in))
    conv_out = inverse_transform(
        corner,
        weight * (in_real * kernel_real + in_imag * kernel_imag),
        weight * (in_imag * kernel_real - in_real * kernel_imag),
    ).reshape(inputs.shape)
    mixed = inputs + conv_out
    second, normed_second, inv_second = norm_forward(mixed, gain_second)
    mlp_in = second.astype(jnp.bfloat16).reshape(-1, channels)
    hidden = jnp.dot(mlp_in, up_weight, preferred_element_type=jnp.float32)
    value, slope = gelu_parts(hidden)
    activated = value.astype(jnp.bfloat16)
    upstream = cotangent.reshape(-1, channels)
    grad_act = lax.dot_general(
        upstream, down_weight, (((1,), (1,)), ((), ())), preferred_element_type=jnp.float32
    )
    grad_hidden = (grad_act * slope).astype(jnp.bfloat16)
    up_rows = lax.dot_general(
        grad_hidden, mlp_in, (((0,), (0,)), ((), ())), preferred_element_type=jnp.float32
    )
    down_rows = lax.dot_general(
        activated, upstream, (((0,), (0,)), ((), ())), preferred_element_type=jnp.float32
    )
    bits = mesh_bits(("gy", "gx", "dp"))
    along = {axis: [pair for pair in bits if pair[0] == axis][::-1] for axis in ("gy", "gx", "dp")}
    near = along["gx"][:1]
    columns_next = near + along["gx"][1:] + along["gy"] + along["dp"]
    rows_next = near + along["gy"] + along["gx"][1:] + along["dp"]
    steps = len(bits)
    up_sum = blocked(up_rows, bits)
    down_sum = blocked(down_rows, bits)

    def up_step(blocks, step):
        return halve(blocks, bits, columns_next, step, jnp.bfloat16) if step < steps else blocks

    def down_step(blocks, step):
        return halve(blocks, bits, rows_next, step, jnp.bfloat16) if step < steps else blocks

    grad_normed = lax.dot_general(
        grad_hidden, up_weight, (((1,), (1,)), ((), ())), preferred_element_type=jnp.float32
    ).reshape(mixed.shape)
    grad_mixed = cotangent.astype(jnp.float32) + norm_backward(
        grad_normed, gain_second, normed_second, inv_second
    )
    grad_conv = grad_mixed.astype(jnp.bfloat16)
    fence = lax.optimization_barrier
    taps = side * side
    up_sum = up_step(up_sum, 0)
    down_sum = down_step(down_sum, 0)
    tall_grad = extend_rows(grad_conv, reach)
    tile_real, tile_imag = forward_transform(corner, flat(grad_conv))
    grad_taps = inverse_transform(
        tap_table,
        weight * jnp.sum(in_real * tile_real + in_imag * tile_imag, axis=0, keepdims=True),
        weight * jnp.sum(in_imag * tile_real - in_real * tile_imag, axis=0, keepdims=True),
    )
    gain_second_sum = jnp.sum(grad_normed * normed_second, axis=(0, 1, 2))
    small = jnp.concatenate(
        [
            grad_taps[0],
            gain_second_sum[None],
            jnp.zeros((-(taps + 1) % (8 << steps), channels), jnp.float32),
        ]
    )
    small = blocked(small, bits)
    tall_grad, small, up_sum, down_sum = fence((tall_grad, small, up_sum, down_sum))

    small = halve(small, columns_next, columns_next, 0, jnp.float32)
    padded_grad = extend_cols(tall_grad, reach)
    up_sum = up_step(up_sum, 1)
    down_sum = down_step(down_sum, 1)
    padded_grad, small, up_sum, down_sum = fence((padded_grad, small, up_sum, down_sum))

    small = halve(small, columns_next, columns_next, 1, jnp.float32)
    up_sum = up_step(up_sum, 2)
    down_sum = down_step(down_sum, 2)
    grad_real, grad_imag = forward_transform(whole, flat(padded_grad))
    product_real = weight * (grad_real * kernel_real - grad_imag * kernel_imag)
    product_imag = weight * (grad_real * kernel_imag + grad_imag * kernel_real)
    product_real, product_imag, small, up_sum, down_sum = fence(
        (
            product_real.astype(jnp.bfloat16),
            product_imag.astype(jnp.bfloat16),
            small,
            up_sum,
            down_sum,
        )
    )

    small = halve(small, columns_next, columns_next, 2, jnp.float32)
    up_sum = up_step(up_sum, 3)
    down_sum = down_step(down_sum, 3)
    grad_source = inverse_transform(shifted, product_real, product_imag).reshape(inputs.shape)
    grad_input = (
        grad_mixed + norm_backward(grad_source, gain_first, normed_first, inv_first)
    ).astype(jnp.bfloat16)
    gain_first_sum = jnp.sum(grad_source * normed_first, axis=(0, 1, 2))[None]
    gain_first_sum, small, up_sum, down_sum = fence((gain_first_sum, small, up_sum, down_sum))

    for step in range(4, steps):
        up_sum = up_step(up_sum, step)
        down_sum = down_step(down_sum, step)
    for step in range(3, steps):
        small = halve(small, columns_next, columns_next, step, jnp.float32)
    for axis, bit in reversed(columns_next):
        small = double(small, axis, bit)
        gain_first_sum = gain_first_sum + swap(gain_first_sum, axis, bit)
    divisor = tile_rows * lax.axis_size("gy")
    return (
        grad_input,
        up_sum / divisor,
        down_sum / divisor,
        small[:taps].reshape(side, side, channels) / divisor,
        gain_first_sum[0] / divisor,
        small[taps] / divisor,
    )


def solution(mesh):
    in_specs = (P("dp", "gy", "gx", None), P(), P(), P(), P(), P(), P("dp", "gy", "gx", None))
    out_specs = (
        P("dp", "gy", "gx", None),
        P(("gy", "gx", "dp"), None),
        P(("gy", "gx", "dp"), None),
        P(),
        P(),
        P(),
    )
    return jax.shard_map(local, mesh=mesh, in_specs=in_specs, out_specs=out_specs, check_vma=False)
```

```python
import jax
import jax.numpy as jnp
import numpy as np
from jax import lax
from jax.sharding import PartitionSpec as P

EPS = 1e-06
GELU_C = 0.7978845608028654
GELU_A = 0.044715


def padded_2(x, sides, width):
    for axis, dim in sides:
        size, length = (lax.axis_size(axis), x.shape[dim])
        up = [(i, (i + 1) % size) for i in range(size - 1)]
        down = [(j, i) for i, j in up]
        last = lax.slice_in_dim(x, length - width, length, axis=dim)
        initial = lax.slice_in_dim(x, 0, width, axis=dim)
        before = lax.ppermute(last, axis, up)
        after = lax.ppermute(initial, axis, down)
        x = jnp.concatenate([before, x, after], axis=dim)
    return x


def gelu_parts(hidden):
    tangent = jnp.tanh(GELU_C * (hidden + GELU_A * hidden * hidden * hidden))
    value = 0.5 * hidden * (1.0 + tangent)
    slope = 0.5 * (1.0 + tangent) + 0.5 * hidden * (1.0 - tangent * tangent) * GELU_C * (
        1.0 + 3.0 * GELU_A * hidden * hidden
    )
    return (value, slope)


def norm_forward(source, gain):
    mean_val = jnp.mean(source, axis=-1, keepdims=True)
    centred = source - mean_val
    spread = jnp.mean(centred * centred, axis=-1, keepdims=True)
    scale_inv = lax.rsqrt(spread + EPS)
    normed = centred * scale_inv
    return (normed * gain, normed, scale_inv)


def norm_backward(upstream, gain, normed, scale_inv):
    scaled = upstream * gain
    return scale_inv * (
        scaled
        - jnp.mean(scaled, axis=-1, keepdims=True)
        - normed * jnp.mean(scaled * normed, axis=-1, keepdims=True)
    )


def extend_rows(source, reach):
    return padded_2(source, (("gy", 1),), reach)


def extend_cols(source, reach):
    wide = padded_2(source, (("gx", 2),), reach)
    return jnp.pad(wide, ((0, 0), (0, 0), (0, -wide.shape[2] % 16), (0, 0)))


def transform_tables(tile_rows, tile_cols, side):
    rows, cols = tile_rows + side - 1, tile_cols + side - 1
    freqs, weight = [], []
    for fx in range(cols // 2 + 1):
        self_paired = 2 * fx % cols == 0
        for fy in range(rows // 2 + 1 if self_paired else rows):
            freqs.append((fy, fx))
            alone = self_paired and 2 * fy % rows == 0
            weight.append((1.0 if alone else 2.0) / (rows * cols))
    freqs = np.array(freqs)

    def table(row_ids, col_ids):
        angle = 2 * np.pi * (
            (freqs[:, :1] * row_ids % rows)[:, :, None] / rows
            + (freqs[:, 1:] * col_ids % cols)[:, None, :] / cols
        )
        angle = angle.reshape(len(freqs), -1)
        return jnp.asarray(np.concatenate([np.cos(angle), -np.sin(angle)]), jnp.bfloat16)

    whole = table(np.arange(rows), np.arange(cols + -cols % 16))
    corner = table(np.arange(tile_rows), np.arange(tile_cols))
    shifted = table(np.arange(tile_rows) + side - 1, np.arange(tile_cols) + side - 1)
    taps = table(np.arange(side), np.arange(side))
    return whole, corner, shifted, taps, np.array(weight, np.float32)[:, None]


def forward_transform(table, values):
    out = jnp.einsum("fp,bpc->bfc", table, values, preferred_element_type=jnp.float32)
    count = table.shape[0] // 2
    return out[:, :count], out[:, count:]


def inverse_transform(table, real, imag):
    spectrum = jnp.concatenate([real, imag], axis=1).astype(jnp.bfloat16)
    return jnp.einsum("fp,bfc->bpc", table, spectrum, preferred_element_type=jnp.float32)


def flat(values):
    return values.reshape(values.shape[0], -1, values.shape[3])


def mesh_bits(axes):
    bits = []
    for axis in axes:
        bit = lax.axis_size(axis) // 2
        while bit:
            bits.append((axis, bit))
            bit //= 2
    return bits


def swap(values, axis, bit):
    size = lax.axis_size(axis)
    return lax.ppermute(values, axis, [(i, i ^ bit) for i in range(size)])


def blocked(values, bits):
    return values.reshape([2] * len(bits) + [values.shape[0] >> len(bits), values.shape[1]])


def halve(blocks, bits, order, step, wire):
    axis, bit = order[step]
    dim = [pair for pair in bits if pair not in order[:step]].index((axis, bit))
    mine = (lax.axis_index(axis) // bit) % 2
    sent = lax.dynamic_index_in_dim(blocks, 1 - mine, dim, keepdims=False).astype(wire)
    kept = lax.dynamic_index_in_dim(blocks, mine, dim, keepdims=False)
    return kept + swap(sent, axis, bit).astype(jnp.float32)


def double(block, axis, bit):
    other = swap(block, axis, bit)
    low = (lax.axis_index(axis) // bit) % 2 == 0
    return jnp.concatenate([jnp.where(low, block, other), jnp.where(low, other, block)], axis=0)


def local(features, gain_first, gain_second, kernel, up_weight, down_weight, cotangent):
    channels = features.shape[3]
    tile_rows = features.shape[1]
    tile_cols = features.shape[2]
    side = kernel.shape[0]
    reach = side // 2
    inputs = features.astype(jnp.float32)
    first, normed_first, inv_first = norm_forward(inputs, gain_first)
    conv_in = first.astype(jnp.bfloat16)
    padded_in = extend_cols(extend_rows(conv_in, reach), reach)
    whole, corner, shifted, tap_table, weight = transform_tables(tile_rows, tile_cols, side)
    kernel_real, kernel_imag = forward_transform(
        tap_table, kernel.reshape(1, side * side, channels).astype(jnp.bfloat16)
    )
    in_real, in_imag = forward_transform(whole, flat(padded_in))
    conv_out = inverse_transform(
        corner,
        weight * (in_real * kernel_real + in_imag * kernel_imag),
        weight * (in_imag * kernel_real - in_real * kernel_imag),
    ).reshape(inputs.shape)
    mixed = inputs + conv_out
    second, normed_second, inv_second = norm_forward(mixed, gain_second)
    mlp_in = second.astype(jnp.bfloat16).reshape(-1, channels)
    hidden = jnp.dot(mlp_in, up_weight, preferred_element_type=jnp.float32)
    value, slope = gelu_parts(hidden)
    activated = value.astype(jnp.bfloat16)
    upstream = cotangent.reshape(-1, channels)
    grad_act = lax.dot_general(
        upstream, down_weight, (((1,), (1,)), ((), ())), preferred_element_type=jnp.float32
    )
    grad_hidden = (grad_act * slope).astype(jnp.bfloat16)
    up_rows = lax.dot_general(
        grad_hidden, mlp_in, (((0,), (0,)), ((), ())), preferred_element_type=jnp.float32
    )
    down_rows = lax.dot_general(
        activated, upstream, (((0,), (0,)), ((), ())), preferred_element_type=jnp.float32
    )
    bits = mesh_bits(("gy", "gx", "dp"))
    along = {axis: [pair for pair in bits if pair[0] == axis][::-1] for axis in ("gy", "gx", "dp")}
    near = along["gx"][:1]
    columns_next = near + along["gx"][1:] + along["gy"] + along["dp"]
    rows_next = near + along["gy"] + along["gx"][1:] + along["dp"]
    steps = len(bits)
    up_sum = blocked(up_rows, bits)
    down_sum = blocked(down_rows, bits)

    def up_step(blocks, step):
        return halve(blocks, bits, columns_next, step, jnp.bfloat16) if step < steps else blocks

    def down_step(blocks, step):
        return halve(blocks, bits, rows_next, step, jnp.bfloat16) if step < steps else blocks

    grad_normed = lax.dot_general(
        grad_hidden, up_weight, (((1,), (1,)), ((), ())), preferred_element_type=jnp.float32
    ).reshape(mixed.shape)
    grad_mixed = cotangent.astype(jnp.float32) + norm_backward(
        grad_normed, gain_second, normed_second, inv_second
    )
    grad_conv = grad_mixed.astype(jnp.bfloat16)
    fence = lax.optimization_barrier
    taps = side * side
    up_sum = up_step(up_sum, 0)
    down_sum = down_step(down_sum, 0)
    tall_grad = extend_rows(grad_conv, reach)
    tile_real, tile_imag = forward_transform(corner, flat(grad_conv))
    grad_taps = inverse_transform(
        tap_table,
        weight * jnp.sum(in_real * tile_real + in_imag * tile_imag, axis=0, keepdims=True),
        weight * jnp.sum(in_imag * tile_real - in_real * tile_imag, axis=0, keepdims=True),
    )
    gain_second_sum = jnp.sum(grad_normed * normed_second, axis=(0, 1, 2))
    small = jnp.concatenate(
        [
            grad_taps[0],
            gain_second_sum[None],
            jnp.zeros((-(taps + 1) % (8 << steps), channels), jnp.float32),
        ]
    )
    small = blocked(small, bits)
    tall_grad, small, up_sum, down_sum = fence((tall_grad, small, up_sum, down_sum))

    small = halve(small, columns_next, columns_next, 0, jnp.float32)
    padded_grad = extend_cols(tall_grad, reach)
    up_sum = up_step(up_sum, 1)
    down_sum = down_step(down_sum, 1)
    padded_grad, small, up_sum, down_sum = fence((padded_grad, small, up_sum, down_sum))

    small = halve(small, columns_next, columns_next, 1, jnp.float32)
    up_sum = up_step(up_sum, 2)
    down_sum = down_step(down_sum, 2)
    grad_real, grad_imag = forward_transform(whole, flat(padded_grad))
    product_real = weight * (grad_real * kernel_real - grad_imag * kernel_imag)
    product_imag = weight * (grad_real * kernel_imag + grad_imag * kernel_real)
    product_real, product_imag, small, up_sum, down_sum = fence(
        (
            product_real.astype(jnp.bfloat16),
            product_imag.astype(jnp.bfloat16),
            small,
            up_sum,
            down_sum,
        )
    )

    small = halve(small, columns_next, columns_next, 2, jnp.float32)
    up_sum = up_step(up_sum, 3)
    down_sum = down_step(down_sum, 3)
    grad_source = inverse_transform(shifted, product_real, product_imag).reshape(inputs.shape)
    grad_input = (
        grad_mixed + norm_backward(grad_source, gain_first, normed_first, inv_first)
    ).astype(jnp.bfloat16)
    gain_first_sum = jnp.sum(grad_source * normed_first, axis=(0, 1, 2))[None]
    gain_first_sum, small, up_sum, down_sum = fence((gain_first_sum, small, up_sum, down_sum))

    rest = [pair for pair in reversed(columns_next)]
    summed = 0
    for step in range(3, steps):
        small = halve(small, columns_next, columns_next, step, jnp.float32)
        up_sum = up_step(up_sum, step + 1)
        down_sum = down_step(down_sum, step + 1)
        if step > 3 or steps < 5:
            gain_first_sum = gain_first_sum + swap(gain_first_sum, *rest[summed])
            summed += 1
        small, gain_first_sum, up_sum, down_sum = fence((small, gain_first_sum, up_sum, down_sum))
    for axis, bit in rest:
        small = double(small, axis, bit)
        if summed < steps:
            gain_first_sum = gain_first_sum + swap(gain_first_sum, *rest[summed])
            summed += 1
        small, gain_first_sum = fence((small, gain_first_sum))
    divisor = tile_rows * lax.axis_size("gy")
    return (
        grad_input,
        up_sum / divisor,
        down_sum / divisor,
        small[:taps].reshape(side, side, channels) / divisor,
        gain_first_sum[0] / divisor,
        small[taps] / divisor,
    )


def solution(mesh):
    in_specs = (P("dp", "gy", "gx", None), P(), P(), P(), P(), P(), P("dp", "gy", "gx", None))
    out_specs = (
        P("dp", "gy", "gx", None),
        P(("gy", "gx", "dp"), None),
        P(("gy", "gx", "dp"), None),
        P(),
        P(),
        P(),
    )
    return jax.shard_map(local, mesh=mesh, in_specs=in_specs, out_specs=out_specs, check_vma=False)
```
